128 devices in a mesh: grp: 16 (over z, y), own: 8 (over x, core).
Axes of the slice: x: 4, y: 4, z: 4, core: 2. Of those that a mesh axis runs over, the one named last changes fastest.
Arguments:
- queries: bfloat16 [4096, 1024], P(('grp', 'own')), may hold values from -20 to 20
- centroids: bfloat16 [32768, 1024], P('own'), may hold values from -6 to 6
- cluster_ids: int32 [4096, 8], P(('grp', 'own')), may hold values from 0 to 255, all different within a row; in each aligned block of 32 rows (0 to 31, 32 to 63, ...) at most 2 rows name the same one
- label_weights: bfloat16 [256, 3072, 1024], P(('grp', 'own')), may hold values from -6 to 6
Outputs:
- label_logp: float32 [4096, 8, 3072], P(('grp', 'own'))
The draws below stay inside these ranges and needn't reach their ends.
Inputs may be any that keep to these rules, and one draw needn't show every extreme that they name: `cluster_ids`: each row names 8 different clusters; among the rows of one device no cluster is named by more than 2 rows, a bound that some block reaches.
All inputs are finite; a program needn't handle non-finite values.
Results may differ from the reference program's by a relative error of at most 0.0003.
Values may be sent and summed in bfloat16 or wider, within the bound.
No kernel may reach another device: no remote copies, remote signals or barrier semaphores. Data moves between devices by JAX's collectives and lax.ppermute only.
A program may use at most 128 MiB of HBM per device.

```python
import math
import jax
import jax.numpy as jnp
import numpy as np
from jax import lax

D = 1024
NCENT = 32768
LB = 3072
TOP = 8
QD = 32
Q = 4096
KW = 256
STRIDE = 128
MOST = 2
N_GRP = 16
N_OWN = 8


def draw_queries(key, part):
    key = jax.random.fold_in(key, 11)
    key_base = jax.random.fold_in(key, 0)
    base = jnp.clip(jax.random.normal(key_base, (Q, D), jnp.float32), -4.0, 4.0)
    values = base
    return values.astype(jnp.bfloat16)


def draw_centroids(key, part):
    key = jax.random.fold_in(key, 23)
    key_base, key_scale = jax.random.split(key, 2)
    base = jnp.clip(jax.random.normal(key_base, (NCENT, D), jnp.float32), -4.0, 4.0) / math.sqrt(D)
    scale = jnp.exp(jax.random.uniform(key_scale, (NCENT, 1), jnp.float32, math.log(0.5), math.log(4.0)))
    values = base * scale
    return values.astype(jnp.bfloat16)


def draw_label_weights(key, part):
    key = jax.random.fold_in(key, 37)
    key_base, key_scale = jax.random.split(key, 2)
    base = jnp.clip(jax.random.normal(key_base, (KW, LB, D), jnp.float32), -4.0, 4.0) / math.sqrt(D)
    scale = jnp.exp(jax.random.uniform(key_scale, (KW, LB, 1), jnp.float32, math.log(0.5), math.log(2.0)))
    values = base * scale
    return values.astype(jnp.bfloat16)


def routed_block(rng, own, number, rows, amount, top, most, skew):
    order = jax.random.permutation(rng, amount)
    packed, common = shares(amount, rows * top, most, skew, True), shares(amount, rows * top, most, skew, False)
    places = jnp.arange(amount)

    def named(tallies, turn):
        used = int((tallies > 0).sum())
        fixed = max(1, used // 4)
        passed = fixed + (places - fixed + turn * (used - fixed)) % max(1, amount - fixed)
        return jnp.zeros((amount,), jnp.int32).at[order[jnp.where(places < fixed, places, passed)]].set(jnp.asarray(tallies, jnp.int32))

    tallies = jnp.where(number % 4 == 0, named(packed, number // 4), named(common, number - number // 4 - 1))
    mixed = jax.random.permutation(jax.random.fold_in(own, 3), amount)
    donor, taker = mixed[0:amount // 2 * 2:2], mixed[1:amount // 2 * 2:2]
    margin = jnp.minimum(tallies[donor] - 1, most - tallies[taker]) // 2
    margin = jnp.where((donor == order[0]) | (taker == order[0]) | (tallies[taker] == 0), 0, jnp.maximum(margin, 0))
    passed = jax.random.randint(jax.random.fold_in(own, 4), (amount // 2,), 0, 1 << 20) % (margin + 1)
    tallies = tallies.at[donor].add(-passed).at[taker].add(passed)
    labels = jnp.searchsorted(jnp.cumsum(tallies), jnp.arange(rows * top), side="right").astype(jnp.int32)
    table = labels.reshape(top, rows).T
    table = table[jax.random.permutation(jax.random.fold_in(own, 1), rows)]
    turn = jax.random.randint(jax.random.fold_in(own, 2), (rows, 1), 0, top)
    return jnp.take_along_axis(table, (jnp.arange(top)[None, :] + turn) % top, axis=1)


def shares(number_of, total, bound, slope, full):
    loads = [(1 << 20) // math.isqrt(standing ** slope) + 1 for standing in range(1, number_of + 1)]
    largest = bound if full else min(bound, max(-(-total // number_of), total * loads[0] // sum(loads)))
    least = 1 if total - largest >= number_of - 1 else 0
    holding, spare = [largest] + [least] * (number_of - 1), total - largest - least * (number_of - 1)
    while spare > 0:
        candidates = [i for i in range(1, number_of) if holding[i] < largest] or [i for i in range(1, number_of) if holding[i] < bound]
        mass, left = sum([loads[i] for i in candidates]), spare
        for i in candidates:
            addition = min(bound - holding[i], max(1, left * loads[i] // mass), spare)
            holding[i] = holding[i] + addition
            spare = spare - addition
    return np.array(holding)


def setup_inputs(seed: int = 0) -> dict:
    streams_of = jax.random.split(jax.random.key(seed), 5)
    queries = draw_queries(jax.random.fold_in(streams_of[4], 71), 0)
    centroids = draw_centroids(jax.random.fold_in(streams_of[4], 71), 0)
    cluster_ids_keys = jax.random.split(jax.random.fold_in(streams_of[2], 1), Q // QD)
    cluster_ids_turns = jax.random.permutation(jax.random.fold_in(streams_of[2], 3), Q // QD)
    cluster_ids = jax.vmap(lambda own, number: routed_block(jax.random.fold_in(streams_of[2], 2), own, number, QD, KW, TOP, MOST, 2))(cluster_ids_keys, cluster_ids_turns).reshape((Q, TOP))
    label_weights = draw_label_weights(jax.random.fold_in(streams_of[4], 71), 0)
    return {"queries": queries, "centroids": centroids, "cluster_ids": cluster_ids, "label_weights": label_weights}


def reference(queries, centroids, cluster_ids, label_weights):
    devices = N_GRP * N_OWN
    blocks = QD * N_OWN
    chosen = cluster_ids * STRIDE

    def prior_block(pair):
        query_block, chosen_block = pair
        scores = jnp.dot(query_block, centroids.T, preferred_element_type=jnp.float32)
        largest = jnp.max(scores, axis=1)
        normalizer = largest + jnp.log(jnp.sum(jnp.exp(scores - largest[:, None]), axis=1))
        picked = jnp.take_along_axis(scores, chosen_block, axis=1)
        return picked - normalizer[:, None]

    prior = lax.map(prior_block, (queries.reshape(Q // blocks, blocks, D), chosen.reshape(Q // blocks, blocks, TOP)))
    prior = prior.reshape(Q, TOP)

    clusters = jnp.arange(KW, dtype=jnp.int32)
    member = jnp.any(cluster_ids[:, :, None] == clusters[None, None, :], axis=1).astype(jnp.int32)
    member = member.reshape(devices, QD, KW)
    ranks = (jnp.cumsum(member, axis=1) - member).astype(jnp.int32)
    slot_rank = jnp.take_along_axis(ranks.reshape(Q, KW), cluster_ids, axis=1).astype(jnp.int32)
    query_blocks = queries.reshape(devices, QD, D).astype(jnp.float32)
    places = jnp.arange(MOST, dtype=jnp.int32)

    def cluster_scores(cluster):
        present = member[:, :, cluster]
        order = ranks[:, :, cluster]
        select = ((order[:, None, :] == places[None, :, None]) & (present[:, None, :] == 1)).astype(jnp.float32)
        routed = jnp.einsum('vmq,vqd->vmd', select, query_blocks).reshape(devices * MOST, D).astype(jnp.bfloat16)
        weight = label_weights[cluster]
        logits = jnp.dot(routed, weight.T, preferred_element_type=jnp.float32)
        largest = jnp.max(logits, axis=1)
        log_total = largest + jnp.log(jnp.sum(jnp.exp(logits - largest[:, None]), axis=1))
        return logits.astype(jnp.bfloat16), log_total

    label_scores, block_total = lax.map(cluster_scores, clusters)
    source = (jnp.arange(Q, dtype=jnp.int32) // QD)[:, None]
    flat_index = (cluster_ids * (devices * MOST) + source * MOST + slot_rank).reshape(-1)
    picked = jnp.take(label_scores.reshape(KW * devices * MOST, LB), flat_index, axis=0)
    picked = picked.reshape(Q, TOP, LB).astype(jnp.float32)
    totals = jnp.take(block_total.reshape(-1), flat_index).reshape(Q, TOP)
    return prior[:, :, None] + picked - totals[:, :, None]
```

```python
import functools

import jax
import jax.numpy as jnp
from jax import lax
from jax.experimental import pallas as pl
from jax.experimental.pallas import tpu as pltpu
from jax.sharding import PartitionSpec as P

LANES = 128
F32, BF16 = jnp.float32, jnp.bfloat16
MIB = 1 << 20


def route_kernel(clusters, capacity, queries_hbm, ids_hbm, out_ref, slot_ref, queries_ref, ids_ref, stage, sems):
    copies = [
        pltpu.make_async_copy(ids_hbm, ids_ref, sems.at[0]),
        pltpu.make_async_copy(queries_hbm, queries_ref, sems.at[1]),
    ]
    for copy in copies:
        copy.start()
    copies[0].wait()
    rows, width = queries_ref.shape
    beam = ids_ref.shape[0]
    tiles = width // LANES
    cluster = lax.broadcasted_iota(jnp.int32, (clusters, rows), 0)
    named = [cluster == ids_ref[s : s + 1, :] for s in range(beam)]
    hits = functools.reduce(jnp.logical_or, named)
    earlier = lax.broadcasted_iota(jnp.int32, (rows, rows), 0) < lax.broadcasted_iota(
        jnp.int32, (rows, rows), 1
    )
    before = jnp.dot(
        jnp.where(hits, 1.0, 0.0).astype(BF16),
        jnp.where(earlier, 1.0, 0.0).astype(BF16),
        preferred_element_type=F32,
    )
    copies[1].wait()
    for m in range(capacity):
        select = jnp.where(hits & (before == m), 1.0, 0.0).astype(BF16)
        routed = jnp.dot(select, queries_ref[...], preferred_element_type=F32)
        for k in range(tiles):
            stage[pl.ds(m * tiles + k, clusters, stride=capacity * tiles), :] = routed[
                :, k * LANES : (k + 1) * LANES
            ]
    out_ref[...] = stage[...].astype(BF16)
    rank = jnp.concatenate(
        [jnp.sum(jnp.where(n, before, 0.0), axis=0, keepdims=True) for n in named], axis=0
    )
    slot_ref[...] = ids_ref[...] * capacity + rank.astype(jnp.int32)


def route(queries, ids, clusters, capacity):
    rows, width = queries.shape
    total = clusters * capacity * width // LANES
    return pl.pallas_call(
        functools.partial(route_kernel, clusters, capacity),
        out_shape=(
            jax.ShapeDtypeStruct((total, LANES), BF16),
            jax.ShapeDtypeStruct(ids.shape, jnp.int32),
        ),
        in_specs=[pl.BlockSpec(memory_space=pltpu.HBM)] * 2,
        scratch_shapes=[
            pltpu.VMEM(queries.shape, BF16),
            pltpu.VMEM(ids.shape, jnp.int32),
            pltpu.VMEM((total, LANES), F32),
            pltpu.SemaphoreType.DMA((2,)),
        ],
        compiler_params=pltpu.CompilerParams(vmem_limit_bytes=56 * MIB),
        name="route",
    )(queries, ids)


def label_kernel(sources, capacity, arrived_ref, weights_ref, out_ref, spread, x, w, logits, stage, pack, sems, out_sems):
    held, labels, width = weights_ref.shape
    tiles, columns = width // LANES, labels // LANES
    rows = stage.shape[0] // sources
    blocks = w.shape[1]
    block = labels // blocks
    here = block // LANES
    parts = out_sems.shape[0]
    count = sources // parts

    copies = {
        (c, n): pltpu.make_async_copy(weights_ref.at[c, pl.ds(n * block, block)], w.at[c, n], sems.at[c, n])
        for c in range(held)
        for n in range(blocks)
    }
    for copy in copies.values():
        copy.start()
    spread[...] = arrived_ref[...].astype(F32)

    def gather(c):
        for m in range(capacity):
            for k in range(tiles):
                x[c, m * sources : (m + 1) * sources, k * LANES : (k + 1) * LANES] = spread[
                    pl.ds((c * capacity + m) * tiles + k, sources, stride=held * capacity * tiles), :
                ].astype(BF16)

    def product(c, n):
        copies[c, n].wait()
        scores = lax.dot_general(x[c], w[c, n], (((1,), (1,)), ((), ())), preferred_element_type=F32)
        logits[c, :, n * block : (n + 1) * block] = scores
        for m in range(capacity):
            for j in range(here):
                stage[pl.ds((c * capacity + m) * columns + n * here + j, sources, stride=rows), :] = scores[
                    m * sources : (m + 1) * sources, j * LANES : (j + 1) * LANES
                ]

    def total(c, m, p):
        scores = logits[c, m * sources + p * count : m * sources + (p + 1) * count, :]
        largest = jnp.max(scores, axis=1, keepdims=True)
        return largest + jnp.log(jnp.sum(jnp.exp(scores - largest), axis=1, keepdims=True))

    totals = {}
    places = held * capacity
    for c in range(held):
        gather(c)
        for n in range(blocks):
            product(c, n)
            if c > 0:
                for p in range(n * parts // blocks, (n + 1) * parts // blocks):
                    for m in range(capacity):
                        totals[c - 1, m, p] = total(c - 1, m, p)

    lane = lax.broadcasted_iota(jnp.int32, (count, LANES), 1)
    outs = []
    for p in range(parts):
        for m in range(capacity):
            totals[held - 1, m, p] = total(held - 1, m, p)
        packed = jnp.zeros((count, LANES), F32)
        for c in range(held):
            for m in range(capacity):
                rest = totals[c, m, p]
                for t in range(3):
                    term = rest.astype(BF16).astype(F32)
                    packed = jnp.where(lane == t * places + c * capacity + m, term, packed)
                    rest = rest - term
        stage[pl.ds(p * count * rows + places * columns, count, stride=rows), :] = packed
        stage[pl.ds(p * count * rows + places * columns + 1, count, stride=rows), :] = jnp.zeros_like(packed)
        span = pl.ds(p * count * rows, count * rows)
        pack[span, :] = stage[span, :].astype(BF16)
        out = pltpu.make_async_copy(pack.at[span], out_ref.at[span], out_sems.at[p])
        out.start()
        outs.append(out)
    for out in outs:
        out.wait()


def score_labels(arrived, weights, sources, capacity):
    held, labels, width = weights.shape
    slots = sources * capacity
    blocks = 2
    rows = held * capacity * labels // LANES + 2
    return pl.pallas_call(
        functools.partial(label_kernel, sources, capacity),
        in_specs=[pl.BlockSpec(memory_space=pltpu.VMEM), pl.BlockSpec(memory_space=pltpu.HBM)],
        out_specs=pl.BlockSpec(memory_space=pltpu.HBM),
        out_shape=jax.ShapeDtypeStruct((sources * rows, LANES), BF16),
        scratch_shapes=[
            pltpu.VMEM(arrived.shape, F32),
            pltpu.VMEM((held, slots, width), BF16),
            pltpu.VMEM((held, blocks, labels // blocks, width), BF16),
            pltpu.VMEM((held, slots, labels), F32),
            pltpu.VMEM((sources * rows, LANES), F32),
            pltpu.VMEM((sources * rows, LANES), BF16),
            pltpu.SemaphoreType.DMA((held, blocks)),
            pltpu.SemaphoreType.DMA((4,)),
        ],
        compiler_params=pltpu.CompilerParams(vmem_limit_bytes=54 * MIB),
        cost_estimate=pl.CostEstimate(
            flops=2 * held * slots * labels * width,
            bytes_accessed=2 * held * labels * width,
            transcendentals=held * slots * labels,
        ),
        name="score_labels",
    )(arrived, weights)


def centroid_kernel(spacing, *refs):
    chips = (len(refs) - 7) // 2
    mine_refs, theirs_ref, centroids_ref, out_refs = refs[:chips], refs[chips], refs[chips + 1], refs[chips + 2 : -5]
    x, w, scores, heads, sems = refs[-5:]
    blocks, block, _ = w.shape
    here = block // spacing
    held = heads.shape[0]
    rows = mine_refs[0].shape[0]
    copies = [
        pltpu.make_async_copy(centroids_ref.at[pl.ds(n * block, block)], w.at[n], sems.at[n]) for n in range(blocks)
    ]
    for copy in copies:
        copy.start()
    for i, ref in enumerate(mine_refs):
        x[2 * i * rows : (2 * i + 1) * rows, :] = ref[...]
        x[(2 * i + 1) * rows : (2 * i + 2) * rows, :] = theirs_ref[i * rows : (i + 1) * rows, :]
    for n in range(blocks):
        copies[n].wait()
        scores[:, n * block : (n + 1) * block] = lax.dot_general(
            x[...], w[n], (((1,), (1,)), ((), ())), preferred_element_type=F32
        )
        for h in range(here):
            heads[n * here + h : n * here + h + 1, :] = w[n, h * spacing : h * spacing + 16, :].astype(F32)[0:1]
    picked = lax.dot_general(x[...], heads[...].astype(BF16), (((1,), (1,)), ((), ())), preferred_element_type=F32)
    lane = lax.broadcasted_iota(jnp.int32, (2 * rows, LANES), 1)
    for i, ref in enumerate(out_refs):
        span = slice(2 * i * rows, 2 * (i + 1) * rows)
        part = scores[span, :]
        largest = jnp.max(part, axis=1, keepdims=True)
        summed = jnp.sum(jnp.exp(part - largest), axis=1, keepdims=True)
        padded = jnp.concatenate([picked[span], jnp.zeros((2 * rows, LANES - held), F32)], axis=1)
        ref[...] = jnp.where(lane == held, largest, jnp.where(lane == held + 1, summed, padded))


def score_centroids(mine, theirs, centroids, spacing):
    rows, width = mine[0].shape
    held = centroids.shape[0]
    chips = len(mine)
    total = 2 * rows * chips
    blocks = 2
    whole = pl.BlockSpec(memory_space=pltpu.VMEM)
    return pl.pallas_call(
        functools.partial(centroid_kernel, spacing),
        in_specs=[whole] * (chips + 1) + [pl.BlockSpec(memory_space=pltpu.HBM)],
        out_specs=[whole] * chips,
        out_shape=[jax.ShapeDtypeStruct((2 * rows, LANES), F32)] * chips,
        scratch_shapes=[
            pltpu.VMEM((total, width), BF16),
            pltpu.VMEM((blocks, held // blocks, width), BF16),
            pltpu.VMEM((total, held), F32),
            pltpu.VMEM((held // spacing, width), F32),
            pltpu.SemaphoreType.DMA((blocks,)),
        ],
        compiler_params=pltpu.CompilerParams(vmem_limit_bytes=54 * MIB),
        cost_estimate=pl.CostEstimate(
            flops=2 * total * held * width, bytes_accessed=2 * held * width, transcendentals=total * held
        ),
        name="score_centroids",
    )(*mine, theirs, centroids)


def prior_kernel(heads, owner_ref, ids_ref, *refs):
    *share_refs, out_ref = refs
    beam, rows, _ = out_ref.shape
    lane = lax.broadcasted_iota(jnp.int32, (rows, LANES), 1)
    shares = [ref[i * rows : (i + 1) * rows, :] for ref in share_refs for i in range(ref.shape[0] // rows)]
    largest = functools.reduce(jnp.maximum, [v[:, heads : heads + 1] for v in shares])
    summed = sum(v[:, heads + 1 : heads + 2] * jnp.exp(v[:, heads : heads + 1] - largest) for v in shares)
    normalizer = largest + jnp.log(summed)
    ids = ids_ref[...]
    for s in range(beam):
        here = jnp.zeros((rows, LANES), F32)
        for o, v in enumerate(shares):
            at = ids[:, s : s + 1] - owner_ref[o] * heads
            here += jnp.where((lane == at) & (lane < heads), v, 0.0)
        picked = jnp.sum(here, axis=1, keepdims=True)
        out_ref[s] = jnp.broadcast_to(picked - normalizer, (rows, LANES))


def priors(owners, ids, shares, heads):
    rows, beam = ids.shape
    whole = pl.BlockSpec(memory_space=pltpu.VMEM)
    return pl.pallas_call(
        functools.partial(prior_kernel, heads),
        in_specs=[pl.BlockSpec(memory_space=pltpu.SMEM)] + [whole] * (1 + len(shares)),
        out_specs=whole,
        out_shape=jax.ShapeDtypeStruct((beam, rows, LANES), F32),
        compiler_params=pltpu.CompilerParams(vmem_limit_bytes=4 * MIB),
        name="priors",
    )(owners, ids, *shares)


def join_kernel(capacity, columns, slot_ref, prior_ref, scores_ref, out_ref, total_b, wide, ready, sems):
    beam, queries, _ = prior_ref.shape
    per_owner, sources, _ = total_b.shape
    rows = scores_ref.shape[0] // sources
    spans = 8
    span = scores_ref.shape[0] // spans
    for i in range(spans):
        wide[i * span : (i + 1) * span, :] = scores_ref[i * span : (i + 1) * span, :].astype(F32)
    terms = wide[pl.ds(per_owner * columns, sources, stride=rows), :]
    for j in range(per_owner):
        total = sum(terms[:, t * per_owner + j : t * per_owner + j + 1] for t in range(3))
        total_b[j] = jnp.broadcast_to(total, (sources, LANES))

    parts = sems.shape[0]
    block = queries // parts

    def copy(g):
        here = pl.ds(pl.multiple_of(g * block * beam * columns, 8), block * beam * columns)
        return pltpu.make_async_copy(ready.at[here], out_ref.at[here], sems.at[g])

    @pl.loop(0, parts)
    def _(g):
        for i in range(block):
            q = g * block + i
            for s in range(beam):
                slot = slot_ref[s, q]
                source = slot // per_owner
                place = slot % per_owner
                row = wide[pl.ds(source * rows + place * columns, columns), :]
                shift = prior_ref[s, pl.ds(q, 1), :] - total_b[place, pl.ds(source, 1), :]
                ready[pl.ds(q * beam * columns + s, columns, stride=beam), :] = row + shift
        copy(g).start()

    @pl.loop(0, parts)
    def _(g):
        copy(g).wait()


def join(slots, prior, scores, capacity, held, labels):
    beam, queries = slots.shape
    columns = labels // LANES
    places = held * capacity
    sources = scores.shape[0] // (places * columns + 2)
    whole = pl.BlockSpec(memory_space=pltpu.VMEM)
    out = pl.pallas_call(
        functools.partial(join_kernel, capacity, columns),
        in_specs=[pl.BlockSpec(memory_space=pltpu.SMEM)] + [whole] * 2,
        out_specs=pl.BlockSpec(memory_space=pltpu.HBM),
        out_shape=jax.ShapeDtypeStruct((queries * beam * columns, LANES), F32),
        scratch_shapes=[
            pltpu.VMEM((places, sources, LANES), F32),
            pltpu.VMEM(scores.shape, F32),
            pltpu.VMEM((queries * beam * columns, LANES), F32),
            pltpu.SemaphoreType.DMA((8,)),
        ],
        compiler_params=pltpu.CompilerParams(vmem_limit_bytes=24 * MIB),
        name="join",
    )(slots, prior, scores)
    return out.reshape(queries, columns, beam, LANES).transpose(0, 2, 1, 3).reshape(queries, beam, labels)


def exchange(x, axes):
    return lax.all_to_all(x, axes, split_axis=0, concat_axis=0, tiled=True)


def shift(x, by):
    owners = lax.axis_size("own")
    return lax.ppermute(x, "own", [(i, (i + by) % owners) for i in range(owners)])


def swap(x):
    return lax.ppermute(x, "own", [(i, i ^ 1) for i in range(lax.axis_size("own"))])


def body(queries, centroids, cluster_ids, label_weights):
    rows, width = queries.shape
    beam = cluster_ids.shape[1]
    owners = lax.axis_size("own")
    devices = lax.axis_size("grp") * owners
    held, labels, _ = label_weights.shape
    clusters = held * devices
    capacity = 2 * rows * beam // clusters
    spacing = centroids.shape[0] * owners // clusters
    heads = centroids.shape[0] // spacing
    everyone = ("grp", "own")
    hops = range(2, owners, 2)

    mine = [queries] + [shift(queries, by) for by in hops]
    outgoing, slots = route(queries, cluster_ids.T, clusters, capacity)
    outgoing, *mine = lax.optimization_barrier((outgoing, *mine))
    arrived = exchange(outgoing, everyone)

    theirs = swap(jnp.concatenate(mine, axis=0))
    shares = score_centroids(mine, theirs, centroids, spacing)
    arrived, _ = lax.optimization_barrier((arrived, shares[0]))
    back = [shares[0]] + [shift(share, -by) for share, by in zip(shares[1:], hops)]

    scores = score_labels(arrived, label_weights, devices, capacity)
    scores, *back = lax.optimization_barrier((scores, *back))
    pairs = labels * held * capacity // LANES // 2 + 1
    scores_home = exchange(scores.reshape(devices, pairs, 2, LANES), everyone).reshape(scores.shape)

    mate = swap(jnp.concatenate([share[rows:] for share in back], axis=0))
    here = lax.axis_index("own")
    steps = jnp.arange(0, owners, 2, dtype=jnp.int32)
    shard = jnp.concatenate([(here + steps) % owners, ((here ^ 1) + steps) % owners]).astype(jnp.int32)
    prior = priors(shard, cluster_ids, [share[:rows] for share in back] + [mate], heads)
    return join(slots, prior, scores_home, capacity, held, labels)


def solution(mesh):
    placed = (
        P(("grp", "own"), None),
        P("own", None),
        P(("grp", "own"), None),
        P(("grp", "own"), None, None),
    )
    return jax.shard_map(
        body, mesh=mesh, in_specs=placed, out_specs=P(("grp", "own"), None, None), check_vma=False
    )
```

```python
import functools

import jax
import jax.numpy as jnp
from jax import lax
from jax.experimental import pallas as pl
from jax.experimental.pallas import tpu as pltpu
from jax.sharding import PartitionSpec as P

LANES = 128
F32, BF16 = jnp.float32, jnp.bfloat16
MIB = 1 << 20


def route_kernel(clusters, capacity, held, columns, queries_hbm, ids_hbm, out_ref, row_ref, total_ref, queries_ref, ids_ref, stage, sems):
    copies = [
        pltpu.make_async_copy(ids_hbm, ids_ref, sems.at[0]),
        pltpu.make_async_copy(queries_hbm, queries_ref, sems.at[1]),
    ]
    for copy in copies:
        copy.start()
    copies[0].wait()
    rows, width = queries_ref.shape
    beam = ids_ref.shape[0]
    tiles = width // LANES
    cluster = lax.broadcasted_iota(jnp.int32, (clusters, rows), 0)
    named = [cluster == ids_ref[s : s + 1, :] for s in range(beam)]
    hits = functools.reduce(jnp.logical_or, named)
    earlier = lax.broadcasted_iota(jnp.int32, (rows, rows), 0) < lax.broadcasted_iota(
        jnp.int32, (rows, rows), 1
    )
    before = jnp.dot(
        jnp.where(hits, 1.0, 0.0).astype(BF16),
        jnp.where(earlier, 1.0, 0.0).astype(BF16),
        preferred_element_type=F32,
    )
    copies[1].wait()
    for m in range(capacity):
        select = jnp.where(hits & (before == m), 1.0, 0.0).astype(BF16)
        routed = jnp.dot(select, queries_ref[...], preferred_element_type=F32)
        for k in range(tiles):
            stage[pl.ds(m * tiles + k, clusters, stride=capacity * tiles), :] = routed[
                :, k * LANES : (k + 1) * LANES
            ]
    out_ref[...] = stage[...].astype(BF16)
    rank = jnp.concatenate(
        [jnp.sum(jnp.where(n, before, 0.0), axis=0, keepdims=True) for n in named], axis=0
    )
    places = held * capacity
    source = ids_ref[...] // held
    place = ids_ref[...] % held * capacity + rank.astype(jnp.int32)
    row_ref[...] = source * (places * columns + 2) + place * columns
    total_ref[...] = place * (clusters // held) + source


def route(queries, ids, clusters, capacity, held, columns):
    rows, width = queries.shape
    total = clusters * capacity * width // LANES
    return pl.pallas_call(
        functools.partial(route_kernel, clusters, capacity, held, columns),
        out_shape=(
            jax.ShapeDtypeStruct((total, LANES), BF16),
            jax.ShapeDtypeStruct(ids.shape, jnp.int32),
            jax.ShapeDtypeStruct(ids.shape, jnp.int32),
        ),
        in_specs=[pl.BlockSpec(memory_space=pltpu.HBM)] * 2,
        scratch_shapes=[
            pltpu.VMEM(queries.shape, BF16),
            pltpu.VMEM(ids.shape, jnp.int32),
            pltpu.VMEM((total, LANES), F32),
            pltpu.SemaphoreType.DMA((2,)),
        ],
        compiler_params=pltpu.CompilerParams(vmem_limit_bytes=56 * MIB),
        name="route",
    )(queries, ids)


def label_kernel(
    sources, capacity, arrived_ref, weights_ref, out_ref, spread, x, w, peak, mass, stage, pack, sems, out_sems
):
    held, labels, width = weights_ref.shape
    tiles, columns = width // LANES, labels // LANES
    rows = stage.shape[0] // sources
    parts = out_sems.shape[0]
    count = sources // parts
    places = held * capacity
    block = 512
    here = block // LANES

    size = labels // sems.shape[1]
    pieces = []
    for c in range(held):
        for i in range(sems.shape[1]):
            part = pl.ds(i * size, size)
            pieces.append((c, i * size, pltpu.make_async_copy(weights_ref.at[c, part], w.at[c, part], sems.at[c, i])))
    ahead = 2
    for *_, copy in pieces[:ahead]:
        copy.start()
    spread[...] = arrived_ref[...].astype(F32)

    def gather(c):
        for m in range(capacity):
            for k in range(tiles):
                x[c, m * sources : (m + 1) * sources, k * LANES : (k + 1) * LANES] = spread[
                    pl.ds((c * capacity + m) * tiles + k, sources, stride=held * capacity * tiles), :
                ].astype(BF16)

    def product(c, first):
        scores = lax.dot_general(
            x[c], w[c, first : first + block, :], (((1,), (1,)), ((), ())), preferred_element_type=F32
        )
        for m in range(capacity):
            for j in range(here):
                stage[pl.ds((c * capacity + m) * columns + first // LANES + j, sources, stride=rows), :] = scores[
                    m * sources : (m + 1) * sources, j * LANES : (j + 1) * LANES
                ]
        cuts = [scores[:, j * LANES : (j + 1) * LANES] for j in range(here)]
        largest = functools.reduce(jnp.maximum, cuts)
        if first > 0:
            before = peak[c]
            largest = jnp.maximum(largest, before)
        summed = sum(jnp.exp(cut - largest) for cut in cuts)
        if first > 0:
            summed = summed + mass[c] * jnp.exp(before - largest)
        peak[c] = largest
        mass[c] = summed

    for i, (c, first, copy) in enumerate(pieces):
        if first == 0:
            gather(c)
        copy.wait()
        for *_, later in pieces[i + ahead : i + ahead + 1]:
            later.start()
        for n in range(size // block):
            product(c, first + n * block)

    lane = lax.broadcasted_iota(jnp.int32, (sources, LANES), 1)
    packed = jnp.zeros((sources, LANES), F32)
    for c in range(held):
        largest = jnp.max(peak[c], axis=1, keepdims=True)
        total = largest + jnp.log(jnp.sum(mass[c] * jnp.exp(peak[c] - largest), axis=1, keepdims=True))
        for m in range(capacity):
            rest = total[m * sources : (m + 1) * sources]
            for t in range(3):
                term = rest.astype(BF16).astype(F32)
                packed = jnp.where(lane == t * places + c * capacity + m, term, packed)
                rest = rest - term
    stage[pl.ds(places * columns, sources, stride=rows), :] = packed
    stage[pl.ds(places * columns + 1, sources, stride=rows), :] = jnp.zeros_like(packed)
    outs = []
    for p in range(parts):
        span = pl.ds(p * count * rows, count * rows)
        pack[span, :] = stage[span, :].astype(BF16)
        out = pltpu.make_async_copy(pack.at[span], out_ref.at[span], out_sems.at[p])
        out.start()
        outs.append(out)
    for out in outs:
        out.wait()


def score_labels(arrived, weights, sources, capacity):
    held, labels, width = weights.shape
    slots = sources * capacity
    rows = held * capacity * labels // LANES + 2
    return pl.pallas_call(
        functools.partial(label_kernel, sources, capacity),
        in_specs=[pl.BlockSpec(memory_space=pltpu.VMEM), pl.BlockSpec(memory_space=pltpu.HBM)],
        out_specs=pl.BlockSpec(memory_space=pltpu.HBM),
        out_shape=jax.ShapeDtypeStruct((sources * rows, LANES), BF16),
        scratch_shapes=[
            pltpu.VMEM(arrived.shape, F32),
            pltpu.VMEM((held, slots, width), BF16),
            pltpu.VMEM(weights.shape, BF16),
            pltpu.VMEM((held, slots, LANES), F32),
            pltpu.VMEM((held, slots, LANES), F32),
            pltpu.VMEM((sources * rows, LANES), F32),
            pltpu.VMEM((sources * rows, LANES), BF16),
            pltpu.SemaphoreType.DMA((held, 2)),
            pltpu.SemaphoreType.DMA((4,)),
        ],
        compiler_params=pltpu.CompilerParams(vmem_limit_bytes=50 * MIB),
        cost_estimate=pl.CostEstimate(
            flops=2 * held * slots * labels * width,
            bytes_accessed=2 * held * labels * width,
            transcendentals=held * slots * labels,
        ),
        name="score_labels",
    )(arrived, weights)


def centroid_kernel(spacing, *refs):
    chips = (len(refs) - 7) // 2
    mine_refs, theirs_ref, centroids_ref, out_refs = refs[:chips], refs[chips], refs[chips + 1], refs[chips + 2 : -5]
    x, w, scores, heads, sems = refs[-5:]
    blocks, block, _ = w.shape
    here = block // spacing
    held = heads.shape[0]
    rows = mine_refs[0].shape[0]
    copies = [
        pltpu.make_async_copy(centroids_ref.at[pl.ds(n * block, block)], w.at[n], sems.at[n]) for n in range(blocks)
    ]
    for copy in copies:
        copy.start()
    for i, ref in enumerate(mine_refs):
        x[2 * i * rows : (2 * i + 1) * rows, :] = ref[...]
        x[(2 * i + 1) * rows : (2 * i + 2) * rows, :] = theirs_ref[i * rows : (i + 1) * rows, :]
    for n in range(blocks):
        copies[n].wait()
        scores[:, n * block : (n + 1) * block] = lax.dot_general(
            x[...], w[n], (((1,), (1,)), ((), ())), preferred_element_type=F32
        )
        for h in range(here):
            heads[n * here + h : n * here + h + 1, :] = w[n, h * spacing : h * spacing + 16, :].astype(F32)[0:1]
    picked = lax.dot_general(x[...], heads[...].astype(BF16), (((1,), (1,)), ((), ())), preferred_element_type=F32)
    lane = lax.broadcasted_iota(jnp.int32, (2 * rows, LANES), 1)
    for i, ref in enumerate(out_refs):
        span = slice(2 * i * rows, 2 * (i + 1) * rows)
        part = scores[span, :]
        largest = jnp.max(part, axis=1, keepdims=True)
        summed = jnp.sum(jnp.exp(part - largest), axis=1, keepdims=True)
        padded = jnp.concatenate([picked[span], jnp.zeros((2 * rows, LANES - held), F32)], axis=1)
        ref[...] = jnp.where(lane == held, largest, jnp.where(lane == held + 1, summed, padded))


def score_centroids(mine, theirs, centroids, spacing):
    rows, width = mine[0].shape
    held = centroids.shape[0]
    chips = len(mine)
    total = 2 * rows * chips
    blocks = 2
    whole = pl.BlockSpec(memory_space=pltpu.VMEM)
    return pl.pallas_call(
        functools.partial(centroid_kernel, spacing),
        in_specs=[whole] * (chips + 1) + [pl.BlockSpec(memory_space=pltpu.HBM)],
        out_specs=[whole] * chips,
        out_shape=[jax.ShapeDtypeStruct((2 * rows, LANES), F32)] * chips,
        scratch_shapes=[
            pltpu.VMEM((total, width), BF16),
            pltpu.VMEM((blocks, held // blocks, width), BF16),
            pltpu.VMEM((total, held), F32),
            pltpu.VMEM((held // spacing, width), F32),
            pltpu.SemaphoreType.DMA((blocks,)),
        ],
        compiler_params=pltpu.CompilerParams(vmem_limit_bytes=54 * MIB),
        cost_estimate=pl.CostEstimate(
            flops=2 * total * held * width, bytes_accessed=2 * held * width, transcendentals=total * held
        ),
        name="score_centroids",
    )(*mine, theirs, centroids)


def prior_kernel(heads, owner_ref, ids_ref, *refs):
    *share_refs, out_ref = refs
    beam, rows, _ = out_ref.shape
    lane = lax.broadcasted_iota(jnp.int32, (rows, LANES), 1)
    shares = [ref[i * rows : (i + 1) * rows, :] for ref in share_refs for i in range(ref.shape[0] // rows)]
    largest = functools.reduce(jnp.maximum, [v[:, heads : heads + 1] for v in shares])
    summed = sum(v[:, heads + 1 : heads + 2] * jnp.exp(v[:, heads : heads + 1] - largest) for v in shares)
    normalizer = largest + jnp.log(summed)
    ids = ids_ref[...]
    for s in range(beam):
        here = jnp.zeros((rows, LANES), F32)
        for o, v in enumerate(shares):
            at = ids[:, s : s + 1] - owner_ref[o] * heads
            here += jnp.where((lane == at) & (lane < heads), v, 0.0)
        picked = jnp.sum(here, axis=1, keepdims=True)
        out_ref[s] = jnp.broadcast_to(picked - normalizer, (rows, LANES))


def priors(owners, ids, shares, heads):
    rows, beam = ids.shape
    whole = pl.BlockSpec(memory_space=pltpu.VMEM)
    return pl.pallas_call(
        functools.partial(prior_kernel, heads),
        in_specs=[pl.BlockSpec(memory_space=pltpu.SMEM)] + [whole] * (1 + len(shares)),
        out_specs=whole,
        out_shape=jax.ShapeDtypeStruct((beam, rows, LANES), F32),
        compiler_params=pltpu.CompilerParams(vmem_limit_bytes=4 * MIB),
        name="priors",
    )(owners, ids, *shares)


def join_kernel(places, columns, row_ref, place_ref, prior_ref, scores_ref, out_ref, totals, wide, ready, sems):
    beam, queries, _ = prior_ref.shape
    rows = places * columns + 2
    sources = scores_ref.shape[0] // rows
    spans = 8
    span = scores_ref.shape[0] // spans
    for i in range(spans):
        wide[i * span : (i + 1) * span, :] = scores_ref[i * span : (i + 1) * span, :].astype(F32)
    terms = wide[pl.ds(places * columns, sources, stride=rows), :]
    for j in range(places):
        total = sum(terms[:, t * places + j : t * places + j + 1] for t in range(3))
        totals[j * sources : (j + 1) * sources, :] = jnp.broadcast_to(total, (sources, LANES))

    parts = sems.shape[0]
    block = queries // parts

    def copy(g):
        here = pl.ds(g * block * beam * columns, block * beam * columns)
        return pltpu.make_async_copy(ready.at[here], out_ref.at[here], sems.at[g])

    for g in range(parts):
        for q in range(g * block, (g + 1) * block):
            for s in range(beam):
                row = wide[pl.ds(row_ref[s, q], columns), :]
                shift = prior_ref[s, q : q + 1, :] - totals[pl.ds(place_ref[s, q], 1), :]
                ready[pl.ds(q * beam * columns + s, columns, stride=beam), :] = row + shift
        copy(g).start()
    for g in range(parts):
        copy(g).wait()


def join(row_of, place_of, prior, scores, places, labels):
    beam, queries = row_of.shape
    columns = labels // LANES
    sources = scores.shape[0] // (places * columns + 2)
    whole = pl.BlockSpec(memory_space=pltpu.VMEM)
    out = pl.pallas_call(
        functools.partial(join_kernel, places, columns),
        in_specs=[pl.BlockSpec(memory_space=pltpu.SMEM)] * 2 + [whole] * 2,
        out_specs=pl.BlockSpec(memory_space=pltpu.HBM),
        out_shape=jax.ShapeDtypeStruct((queries * beam * columns, LANES), F32),
        scratch_shapes=[
            pltpu.VMEM((places * sources, LANES), F32),
            pltpu.VMEM(scores.shape, F32),
            pltpu.VMEM((queries * beam * columns, LANES), F32),
            pltpu.SemaphoreType.DMA((8,)),
        ],
        compiler_params=pltpu.CompilerParams(vmem_limit_bytes=24 * MIB),
        name="join",
    )(row_of, place_of, prior, scores)
    return out.reshape(queries, columns, beam, LANES).transpose(0, 2, 1, 3).reshape(queries, beam, labels)


def exchange(x, axes):
    return lax.all_to_all(x, axes, split_axis=0, concat_axis=0, tiled=True)


def shift(x, by):
    owners = lax.axis_size("own")
    return lax.ppermute(x, "own", [(i, (i + by) % owners) for i in range(owners)])


def swap(x):
    return lax.ppermute(x, "own", [(i, i ^ 1) for i in range(lax.axis_size("own"))])


def body(queries, centroids, cluster_ids, label_weights):
    rows, width = queries.shape
    beam = cluster_ids.shape[1]
    owners = lax.axis_size("own")
    devices = lax.axis_size("grp") * owners
    held, labels, _ = label_weights.shape
    clusters = held * devices
    capacity = 2 * rows * beam // clusters
    spacing = centroids.shape[0] * owners // clusters
    heads = centroids.shape[0] // spacing
    everyone = ("grp", "own")
    hops = range(2, owners, 2)

    mine = [queries] + [shift(queries, by) for by in hops]
    outgoing, row_of, place_of = route(queries, cluster_ids.T, clusters, capacity, held, labels // LANES)
    outgoing, *mine = lax.optimization_barrier((outgoing, *mine))
    arrived = exchange(outgoing, everyone)

    theirs = swap(jnp.concatenate(mine, axis=0))
    shares = score_centroids(mine, theirs, centroids, spacing)
    arrived, _ = lax.optimization_barrier((arrived, shares[0]))
    back = [shares[0]] + [shift(share, -by) for share, by in zip(shares[1:], hops)]

    scores = score_labels(arrived, label_weights, devices, capacity)
    scores, *back = lax.optimization_barrier((scores, *back))
    pairs = labels * held * capacity // LANES // 2 + 1
    scores_home = exchange(scores.reshape(devices, pairs, 2, LANES), everyone).reshape(scores.shape)

    mate = swap(jnp.concatenate([share[rows:] for share in back], axis=0))
    here = lax.axis_index("own")
    steps = jnp.arange(0, owners, 2, dtype=jnp.int32)
    shard = jnp.concatenate([(here + steps) % owners, ((here ^ 1) + steps) % owners]).astype(jnp.int32)
    prior = priors(shard, cluster_ids, [share[:rows] for share in back] + [mate], heads)
    return join(row_of, place_of, prior, scores_home, held * capacity, labels)


def solution(mesh):
    placed = (
        P(("grp", "own"), None),
        P("own", None),
        P(("grp", "own"), None),
        P(("grp", "own"), None, None),
    )
    return jax.shard_map(
        body, mesh=mesh, in_specs=placed, out_specs=P(("grp", "own"), None, None), check_vma=False
    )
```

```python
import functools

import jax
import jax.numpy as jnp
from jax import lax
from jax.experimental import pallas as pl
from jax.experimental.pallas import tpu as pltpu
from jax.sharding import PartitionSpec as P

LANES = 128
F32, BF16 = jnp.float32, jnp.bfloat16
MIB = 1 << 20


def route_kernel(clusters, capacity, held, columns, queries_hbm, ids_hbm, out_ref, row_ref, total_ref, queries_ref, ids_ref, stage, sems):
    copies = [
        pltpu.make_async_copy(ids_hbm, ids_ref, sems.at[0]),
        pltpu.make_async_copy(queries_hbm, queries_ref, sems.at[1]),
    ]
    for copy in copies:
        copy.start()
    copies[0].wait()
    rows, width = queries_ref.shape
    beam = ids_ref.shape[0]
    tiles = width // LANES
    cluster = lax.broadcasted_iota(jnp.int32, (clusters, rows), 0)
    named = [cluster == ids_ref[s : s + 1, :] for s in range(beam)]
    hits = functools.reduce(jnp.logical_or, named)
    earlier = lax.broadcasted_iota(jnp.int32, (rows, rows), 0) < lax.broadcasted_iota(
        jnp.int32, (rows, rows), 1
    )
    before = jnp.dot(
        jnp.where(hits, 1.0, 0.0).astype(BF16),
        jnp.where(earlier, 1.0, 0.0).astype(BF16),
        preferred_element_type=F32,
    )
    copies[1].wait()
    for m in range(capacity):
        select = jnp.where(hits & (before == m), 1.0, 0.0).astype(BF16)
        routed = jnp.dot(select, queries_ref[...], preferred_element_type=F32)
        for k in range(tiles):
            stage[pl.ds(m * tiles + k, clusters, stride=capacity * tiles), :] = routed[
                :, k * LANES : (k + 1) * LANES
            ]
    out_ref[...] = stage[...].astype(BF16)
    rank = jnp.concatenate(
        [jnp.sum(jnp.where(n, before, 0.0), axis=0, keepdims=True) for n in named], axis=0
    )
    places = held * capacity
    source = ids_ref[...] // held
    place = ids_ref[...] % held * capacity + rank.astype(jnp.int32)
    row_ref[...] = source * (places * columns + 2) + place * columns
    total_ref[...] = place * (clusters // held) + source


def route(queries, ids, clusters, capacity, held, columns):
    rows, width = queries.shape
    total = clusters * capacity * width // LANES
    return pl.pallas_call(
        functools.partial(route_kernel, clusters, capacity, held, columns),
        out_shape=(
            jax.ShapeDtypeStruct((total, LANES), BF16),
            jax.ShapeDtypeStruct(ids.shape, jnp.int32),
            jax.ShapeDtypeStruct(ids.shape, jnp.int32),
        ),
        in_specs=[pl.BlockSpec(memory_space=pltpu.HBM)] * 2,
        scratch_shapes=[
            pltpu.VMEM(queries.shape, BF16),
            pltpu.VMEM(ids.shape, jnp.int32),
            pltpu.VMEM((total, LANES), F32),
            pltpu.SemaphoreType.DMA((2,)),
        ],
        compiler_params=pltpu.CompilerParams(vmem_limit_bytes=56 * MIB),
        name="route",
    )(queries, ids)


def label_kernel(
    sources, capacity, arrived_ref, weights_ref, out_ref, spread, x, w, peak, mass, stage, pack, sems, out_sems
):
    held, labels, width = weights_ref.shape
    tiles, columns = width // LANES, labels // LANES
    rows = stage.shape[0] // sources
    parts = out_sems.shape[0]
    count = sources // parts
    places = held * capacity
    block = 512
    here = block // LANES

    size = labels // sems.shape[1]
    pieces = []
    for c in range(held):
        for i in range(sems.shape[1]):
            part = pl.ds(i * size, size)
            pieces.append((c, i * size, pltpu.make_async_copy(weights_ref.at[c, part], w.at[c, part], sems.at[c, i])))
    ahead = 3
    for *_, copy in pieces[:ahead]:
        copy.start()
    spread[...] = arrived_ref[...].astype(F32)

    def gather(c):
        for m in range(capacity):
            for k in range(tiles):
                x[c, m * sources : (m + 1) * sources, k * LANES : (k + 1) * LANES] = spread[
                    pl.ds((c * capacity + m) * tiles + k, sources, stride=held * capacity * tiles), :
                ].astype(BF16)

    def product(c, first):
        scores = lax.dot_general(
            x[c], w[c, first : first + block, :], (((1,), (1,)), ((), ())), preferred_element_type=F32
        )
        for m in range(capacity):
            for j in range(here):
                stage[pl.ds((c * capacity + m) * columns + first // LANES + j, sources, stride=rows), :] = scores[
                    m * sources : (m + 1) * sources, j * LANES : (j + 1) * LANES
                ]
        cuts = [scores[:, j * LANES : (j + 1) * LANES] for j in range(here)]
        largest = functools.reduce(jnp.maximum, cuts)
        if first > 0:
            before = peak[c]
            largest = jnp.maximum(largest, before)
        summed = sum(jnp.exp(cut - largest) for cut in cuts)
        if first > 0:
            summed = summed + mass[c] * jnp.exp(before - largest)
        peak[c] = largest
        mass[c] = summed

    for c in range(held):
        gather(c)
    lane = lax.broadcasted_iota(jnp.int32, (sources, LANES), 1)

    def pack_totals(c, packed):
        largest = jnp.max(peak[c], axis=1, keepdims=True)
        total = largest + jnp.log(jnp.sum(mass[c] * jnp.exp(peak[c] - largest), axis=1, keepdims=True))
        for m in range(capacity):
            rest = total[m * sources : (m + 1) * sources]
            for t in range(3):
                term = rest.astype(BF16).astype(F32)
                packed = jnp.where(lane == t * places + c * capacity + m, term, packed)
                rest = rest - term
        return packed

    packed = jnp.zeros((sources, LANES), F32)
    for i, (c, first, copy) in enumerate(pieces):
        copy.wait()
        for *_, later in pieces[i + ahead : i + ahead + 1]:
            later.start()
        for n in range(size // block):
            product(c, first + n * block)
        if first == 0 and c > 0:
            packed = pack_totals(c - 1, packed)
    packed = pack_totals(held - 1, packed)
    stage[pl.ds(places * columns, sources, stride=rows), :] = packed
    stage[pl.ds(places * columns + 1, sources, stride=rows), :] = jnp.zeros_like(packed)
    outs = []
    for p in range(parts):
        span = pl.ds(p * count * rows, count * rows)
        pack[span, :] = stage[span, :].astype(BF16)
        out = pltpu.make_async_copy(pack.at[span], out_ref.at[span], out_sems.at[p])
        out.start()
        outs.append(out)
    for out in outs:
        out.wait()


def score_labels(arrived, weights, sources, capacity):
    held, labels, width = weights.shape
    slots = sources * capacity
    rows = held * capacity * labels // LANES + 2
    return pl.pallas_call(
        functools.partial(label_kernel, sources, capacity),
        in_specs=[pl.BlockSpec(memory_space=pltpu.VMEM), pl.BlockSpec(memory_space=pltpu.HBM)],
        out_specs=pl.BlockSpec(memory_space=pltpu.HBM),
        out_shape=jax.ShapeDtypeStruct((sources * rows, LANES), BF16),
        scratch_shapes=[
            pltpu.VMEM(arrived.shape, F32),
            pltpu.VMEM((held, slots, width), BF16),
            pltpu.VMEM(weights.shape, BF16),
            pltpu.VMEM((held, slots, LANES), F32),
            pltpu.VMEM((held, slots, LANES), F32),
            pltpu.VMEM((sources * rows, LANES), F32),
            pltpu.VMEM((sources * rows, LANES), BF16),
            pltpu.SemaphoreType.DMA((held, 2)),
            pltpu.SemaphoreType.DMA((8,)),
        ],
        compiler_params=pltpu.CompilerParams(vmem_limit_bytes=50 * MIB),
        cost_estimate=pl.CostEstimate(
            flops=2 * held * slots * labels * width,
            bytes_accessed=2 * held * labels * width,
            transcendentals=held * slots * labels,
        ),
        name="score_labels",
    )(arrived, weights)


def centroid_kernel(spacing, *refs):
    chips = (len(refs) - 7) // 3
    mine_refs, theirs_refs, centroids_ref, out_refs = (
        refs[:chips], refs[chips : 2 * chips], refs[2 * chips], refs[2 * chips + 1 : -6],
    )
    x, w, peak, mass, heads, sems = refs[-6:]
    held = w.shape[0]
    size = held // sems.shape[0]
    block = 512
    pieces = []
    for i in range(sems.shape[0]):
        part = pl.ds(i * size, size)
        pieces.append(pltpu.make_async_copy(centroids_ref.at[part], w.at[part], sems.at[i]))
    ahead = 4
    for copy in pieces[:ahead]:
        copy.start()
    rows = mine_refs[0].shape[0]
    for i in range(chips):
        x[2 * i * rows : (2 * i + 1) * rows, :] = mine_refs[i][...]
        x[(2 * i + 1) * rows : (2 * i + 2) * rows, :] = theirs_refs[i][...]

    def product(first):
        scores = lax.dot_general(
            x[...], w[first : first + block, :], (((1,), (1,)), ((), ())), preferred_element_type=F32
        )
        cuts = [scores[:, j * LANES : (j + 1) * LANES] for j in range(block // LANES)]
        largest = functools.reduce(jnp.maximum, cuts)
        if first > 0:
            before = peak[...]
            largest = jnp.maximum(largest, before)
        summed = sum(jnp.exp(cut - largest) for cut in cuts)
        if first > 0:
            summed = summed + mass[...] * jnp.exp(before - largest)
        peak[...] = largest
        mass[...] = summed
        for h in range(first // spacing, (first + block) // spacing):
            heads[h : h + 1, :] = w[h * spacing : h * spacing + 16, :].astype(F32)[0:1]

    for i, copy in enumerate(pieces):
        copy.wait()
        for later in pieces[i + ahead : i + ahead + 1]:
            later.start()
        for first in range(i * size, (i + 1) * size, block):
            product(first)
    picked = lax.dot_general(x[...], heads[...].astype(BF16), (((1,), (1,)), ((), ())), preferred_element_type=F32)
    largest = jnp.max(peak[...], axis=1, keepdims=True)
    summed = jnp.sum(mass[...] * jnp.exp(peak[...] - largest), axis=1, keepdims=True)
    count = heads.shape[0]
    lane = lax.broadcasted_iota(jnp.int32, peak.shape, 1)
    padded = jnp.concatenate([picked, jnp.zeros((peak.shape[0], LANES - count), F32)], axis=1)
    shares = jnp.where(lane == count, largest, jnp.where(lane == count + 1, summed, padded))
    for i, ref in enumerate(out_refs):
        ref[...] = shares[2 * i * rows : 2 * (i + 1) * rows, :]


def score_centroids(mine, theirs, centroids, spacing):
    rows, width = mine[0].shape
    held = centroids.shape[0]
    chips = len(mine)
    total = 2 * rows * chips
    whole = pl.BlockSpec(memory_space=pltpu.VMEM)
    return pl.pallas_call(
        functools.partial(centroid_kernel, spacing),
        in_specs=[whole] * (2 * chips) + [pl.BlockSpec(memory_space=pltpu.HBM)],
        out_specs=[whole] * chips,
        out_shape=[jax.ShapeDtypeStruct((2 * rows, LANES), F32)] * chips,
        scratch_shapes=[
            pltpu.VMEM((total, width), BF16),
            pltpu.VMEM(centroids.shape, BF16),
            pltpu.VMEM((total, LANES), F32),
            pltpu.VMEM((total, LANES), F32),
            pltpu.VMEM((held // spacing, width), F32),
            pltpu.SemaphoreType.DMA((4,)),
        ],
        compiler_params=pltpu.CompilerParams(vmem_limit_bytes=53 * MIB),
        cost_estimate=pl.CostEstimate(
            flops=2 * total * held * width, bytes_accessed=2 * held * width, transcendentals=total * held
        ),
        name="score_centroids",
    )(*mine, *theirs, centroids)


def prior_kernel(heads, owner_ref, ids_ref, *refs):
    *share_refs, out_ref = refs
    beam, rows, _ = out_ref.shape
    lane = lax.broadcasted_iota(jnp.int32, (rows, LANES), 1)
    shares = [ref[i * rows : (i + 1) * rows, :] for ref in share_refs for i in range(ref.shape[0] // rows)]
    largest = functools.reduce(jnp.maximum, [v[:, heads : heads + 1] for v in shares])
    summed = sum(v[:, heads + 1 : heads + 2] * jnp.exp(v[:, heads : heads + 1] - largest) for v in shares)
    normalizer = largest + jnp.log(summed)
    ids = ids_ref[...]
    for s in range(beam):
        here = jnp.zeros((rows, LANES), F32)
        for o, v in enumerate(shares):
            at = ids[:, s : s + 1] - owner_ref[o] * heads
            here += jnp.where((lane == at) & (lane < heads), v, 0.0)
        picked = jnp.sum(here, axis=1, keepdims=True)
        out_ref[s] = jnp.broadcast_to(picked - normalizer, (rows, LANES))


def priors(owners, ids, shares, heads):
    rows, beam = ids.shape
    whole = pl.BlockSpec(memory_space=pltpu.VMEM)
    return pl.pallas_call(
        functools.partial(prior_kernel, heads),
        in_specs=[pl.BlockSpec(memory_space=pltpu.SMEM)] + [whole] * (1 + len(shares)),
        out_specs=whole,
        out_shape=jax.ShapeDtypeStruct((beam, rows, LANES), F32),
        compiler_params=pltpu.CompilerParams(vmem_limit_bytes=4 * MIB),
        name="priors",
    )(owners, ids, *shares)


def join_kernel(places, columns, row_ref, place_ref, prior_ref, scores_ref, out_ref, totals, wide, ready, sems):
    beam, queries, _ = prior_ref.shape
    rows = places * columns + 2
    sources = scores_ref.shape[0] // rows
    spans = 8
    span = scores_ref.shape[0] // spans
    for i in range(spans):
        wide[i * span : (i + 1) * span, :] = scores_ref[i * span : (i + 1) * span, :].astype(F32)
    terms = wide[pl.ds(places * columns, sources, stride=rows), :]
    for j in range(places):
        total = sum(terms[:, t * places + j : t * places + j + 1] for t in range(3))
        totals[j * sources : (j + 1) * sources, :] = jnp.broadcast_to(total, (sources, LANES))

    parts = sems.shape[0]
    block = queries // parts

    def copy(g):
        here = pl.ds(g * block * beam * columns, block * beam * columns)
        return pltpu.make_async_copy(ready.at[here], out_ref.at[here], sems.at[g])

    for g in range(parts):
        for q in range(g * block, (g + 1) * block):
            for s in range(beam):
                row = wide[pl.ds(row_ref[s, q], columns), :]
                shift = prior_ref[s, q : q + 1, :] - totals[pl.ds(place_ref[s, q], 1), :]
                ready[pl.ds(q * beam * columns + s, columns, stride=beam), :] = row + shift
        copy(g).start()
    for g in range(parts):
        copy(g).wait()


def join(row_of, place_of, prior, scores, places, labels):
    beam, queries = row_of.shape
    columns = labels // LANES
    sources = scores.shape[0] // (places * columns + 2)
    whole = pl.BlockSpec(memory_space=pltpu.VMEM)
    out = pl.pallas_call(
        functools.partial(join_kernel, places, columns),
        in_specs=[pl.BlockSpec(memory_space=pltpu.SMEM)] * 2 + [whole] * 2,
        out_specs=pl.BlockSpec(memory_space=pltpu.HBM),
        out_shape=jax.ShapeDtypeStruct((queries * beam * columns, LANES), F32),
        scratch_shapes=[
            pltpu.VMEM((places * sources, LANES), F32),
            pltpu.VMEM(scores.shape, F32),
            pltpu.VMEM((queries * beam * columns, LANES), F32),
            pltpu.SemaphoreType.DMA((8,)),
        ],
        compiler_params=pltpu.CompilerParams(vmem_limit_bytes=24 * MIB),
        name="join",
    )(row_of, place_of, prior, scores)
    return out.reshape(queries, columns, beam, LANES).transpose(0, 2, 1, 3).reshape(queries, beam, labels)


def exchange(x, axes):
    return lax.all_to_all(x, axes, split_axis=0, concat_axis=0, tiled=True)


def shift(x, by):
    owners = lax.axis_size("own")
    return lax.ppermute(x, "own", [(i, (i + by) % owners) for i in range(owners)])


def swap(x):
    return lax.ppermute(x, "own", [(i, i ^ 1) for i in range(lax.axis_size("own"))])


def body(queries, centroids, cluster_ids, label_weights):
    rows, width = queries.shape
    beam = cluster_ids.shape[1]
    owners = lax.axis_size("own")
    devices = lax.axis_size("grp") * owners
    held, labels, _ = label_weights.shape
    clusters = held * devices
    capacity = 2 * rows * beam // clusters
    spacing = centroids.shape[0] * owners // clusters
    heads = centroids.shape[0] // spacing
    everyone = ("grp", "own")
    hops = range(2, owners, 2)

    mine = [queries] + [shift(queries, by) for by in hops]
    outgoing, row_of, place_of = route(queries, cluster_ids.T, clusters, capacity, held, labels // LANES)
    outgoing, *mine = lax.optimization_barrier((outgoing, *mine))
    arrived = exchange(outgoing, everyone)

    theirs = [swap(piece) for piece in mine]
    shares = score_centroids(mine, theirs, centroids, spacing)
    arrived, _ = lax.optimization_barrier((arrived, shares[0]))
    back = [shares[0]] + [shift(share, -by) for share, by in zip(shares[1:], hops)]

    scores = score_labels(arrived, label_weights, devices, capacity)
    scores, *back = lax.optimization_barrier((scores, *back))
    pairs = labels * held * capacity // LANES // 2 + 1
    scores_home = exchange(scores.reshape(devices, pairs, 2, LANES), everyone).reshape(scores.shape)

    mate = swap(jnp.concatenate([share[rows:] for share in back], axis=0))
    here = lax.axis_index("own")
    steps = jnp.arange(0, owners, 2, dtype=jnp.int32)
    shard = jnp.concatenate([(here + steps) % owners, ((here ^ 1) + steps) % owners]).astype(jnp.int32)
    prior = priors(shard, cluster_ids, [share[:rows] for share in back] + [mate], heads)
    return join(row_of, place_of, prior, scores_home, held * capacity, labels)


def solution(mesh):
    placed = (
        P(("grp", "own"), None),
        P("own", None),
        P(("grp", "own"), None),
        P(("grp", "own"), None, None),
    )
    return jax.shard_map(
        body, mesh=mesh, in_specs=placed, out_specs=P(("grp", "own"), None, None), check_vma=False
    )
```

```python
import functools

import jax
import jax.numpy as jnp
from jax import lax
from jax.experimental import pallas as pl
from jax.experimental.pallas import tpu as pltpu
from jax.sharding import PartitionSpec as P

LANES = 128
F32, BF16 = jnp.float32, jnp.bfloat16
MIB = 1 << 20


def route_kernel(clusters, capacity, queries_hbm, ids_hbm, out_ref, queries_ref, ids_ref, stage, sems):
    copies = [
        pltpu.make_async_copy(ids_hbm, ids_ref, sems.at[0]),
        pltpu.make_async_copy(queries_hbm, queries_ref, sems.at[1]),
    ]
    for copy in copies:
        copy.start()
    copies[0].wait()
    rows, width = queries_ref.shape
    beam = ids_ref.shape[0]
    tiles = width // LANES
    cluster = lax.broadcasted_iota(jnp.int32, (clusters, rows), 0)
    named = [cluster == ids_ref[s : s + 1, :] for s in range(beam)]
    hits = functools.reduce(jnp.logical_or, named)
    earlier = lax.broadcasted_iota(jnp.int32, (rows, rows), 0) < lax.broadcasted_iota(
        jnp.int32, (rows, rows), 1
    )
    before = jnp.dot(
        jnp.where(hits, 1.0, 0.0).astype(BF16),
        jnp.where(earlier, 1.0, 0.0).astype(BF16),
        preferred_element_type=F32,
    )
    copies[1].wait()
    for m in range(capacity):
        select = jnp.where(hits & (before == m), 1.0, 0.0).astype(BF16)
        routed = jnp.dot(select, queries_ref[...], preferred_element_type=F32)
        for k in range(tiles):
            stage[pl.ds(m * tiles + k, clusters, stride=capacity * tiles), :] = routed[
                :, k * LANES : (k + 1) * LANES
            ]
    out_ref[...] = stage[...].astype(BF16)


def place_kernel(clusters, capacity, held, columns, ids_ref, row_ref, total_ref):
    beam, rows = ids_ref.shape
    cluster = lax.broadcasted_iota(jnp.int32, (clusters, rows), 0)
    named = [cluster == ids_ref[s : s + 1, :] for s in range(beam)]
    hits = functools.reduce(jnp.logical_or, named)
    earlier = lax.broadcasted_iota(jnp.int32, (rows, rows), 0) < lax.broadcasted_iota(
        jnp.int32, (rows, rows), 1
    )
    before = jnp.dot(
        jnp.where(hits, 1.0, 0.0).astype(BF16),
        jnp.where(earlier, 1.0, 0.0).astype(BF16),
        preferred_element_type=F32,
    )
    rank = jnp.concatenate(
        [jnp.sum(jnp.where(n, before, 0.0), axis=0, keepdims=True) for n in named], axis=0
    )
    places = held * capacity
    source = ids_ref[...] // held
    place = ids_ref[...] % held * capacity + rank.astype(jnp.int32)
    row_ref[...] = source * (places * columns + 2) + place * columns
    total_ref[...] = place * (clusters // held) + source


def find_places(ids, clusters, capacity, held, columns):
    return pl.pallas_call(
        functools.partial(place_kernel, clusters, capacity, held, columns),
        out_shape=(jax.ShapeDtypeStruct(ids.shape, jnp.int32),) * 2,
        compiler_params=pltpu.CompilerParams(vmem_limit_bytes=4 * MIB),
        name="places",
    )(ids)


def route(queries, ids, clusters, capacity):
    rows, width = queries.shape
    total = clusters * capacity * width // LANES
    return pl.pallas_call(
        functools.partial(route_kernel, clusters, capacity),
        out_shape=jax.ShapeDtypeStruct((total, LANES), BF16),
        in_specs=[pl.BlockSpec(memory_space=pltpu.HBM)] * 2,
        scratch_shapes=[
            pltpu.VMEM(queries.shape, BF16),
            pltpu.VMEM(ids.shape, jnp.int32),
            pltpu.VMEM((total, LANES), F32),
            pltpu.SemaphoreType.DMA((2,)),
        ],
        compiler_params=pltpu.CompilerParams(vmem_limit_bytes=56 * MIB),
        name="route",
    )(queries, ids)


def label_kernel(
    sources, capacity, arrived_ref, weights_ref, out_ref, spread, x, w, peak, mass, stage, pack, sems, out_sems
):
    held, labels, width = weights_ref.shape
    tiles, columns = width // LANES, labels // LANES
    rows = stage.shape[0] // sources
    parts = out_sems.shape[0]
    count = sources // parts
    places = held * capacity
    block = 512
    here = block // LANES

    size = labels // sems.shape[1]
    pieces = []
    for c in range(held):
        for i in range(sems.shape[1]):
            part = pl.ds(i * size, size)
            pieces.append((c, i * size, pltpu.make_async_copy(weights_ref.at[c, part], w.at[c, part], sems.at[c, i])))
    ahead = 3
    for *_, copy in pieces[:ahead]:
        copy.start()
    spread[...] = arrived_ref[...].astype(F32)

    def gather(c):
        for m in range(capacity):
            for k in range(tiles):
                x[c, m * sources : (m + 1) * sources, k * LANES : (k + 1) * LANES] = spread[
                    pl.ds((c * capacity + m) * tiles + k, sources, stride=held * capacity * tiles), :
                ].astype(BF16)

    def product(c, first):
        scores = lax.dot_general(
            x[c], w[c, first : first + block, :], (((1,), (1,)), ((), ())), preferred_element_type=F32
        )
        for m in range(capacity):
            for j in range(here):
                stage[pl.ds((c * capacity + m) * columns + first // LANES + j, sources, stride=rows), :] = scores[
                    m * sources : (m + 1) * sources, j * LANES : (j + 1) * LANES
                ]
        cuts = [scores[:, j * LANES : (j + 1) * LANES] for j in range(here)]
        largest = functools.reduce(jnp.maximum, cuts)
        if first > 0:
            before = peak[c]
            largest = jnp.maximum(largest, before)
        summed = sum(jnp.exp(cut - largest) for cut in cuts)
        if first > 0:
            summed = summed + mass[c] * jnp.exp(before - largest)
        peak[c] = largest
        mass[c] = summed

    for c in range(held):
        gather(c)
    lane = lax.broadcasted_iota(jnp.int32, (sources, LANES), 1)

    def pack_totals(c, packed):
        largest = jnp.max(peak[c], axis=1, keepdims=True)
        total = largest + jnp.log(jnp.sum(mass[c] * jnp.exp(peak[c] - largest), axis=1, keepdims=True))
        for m in range(capacity):
            rest = total[m * sources : (m + 1) * sources]
            for t in range(3):
                term = rest.astype(BF16).astype(F32)
                packed = jnp.where(lane == t * places + c * capacity + m, term, packed)
                rest = rest - term
        return packed

    packed = jnp.zeros((sources, LANES), F32)
    for i, (c, first, copy) in enumerate(pieces):
        copy.wait()
        for *_, later in pieces[i + ahead : i + ahead + 1]:
            later.start()
        for n in range(size // block):
            product(c, first + n * block)
        if first == 0 and c > 0:
            packed = pack_totals(c - 1, packed)
    packed = pack_totals(held - 1, packed)
    stage[pl.ds(places * columns, sources, stride=rows), :] = packed
    stage[pl.ds(places * columns + 1, sources, stride=rows), :] = jnp.zeros_like(packed)
    outs = []
    for p in range(parts):
        span = pl.ds(p * count * rows, count * rows)
        pack[span, :] = stage[span, :].astype(BF16)
        out = pltpu.make_async_copy(pack.at[span], out_ref.at[span], out_sems.at[p])
        out.start()
        outs.append(out)
    for out in outs:
        out.wait()


def score_labels(arrived, weights, sources, capacity):
    held, labels, width = weights.shape
    slots = sources * capacity
    rows = held * capacity * labels // LANES + 2
    return pl.pallas_call(
        functools.partial(label_kernel, sources, capacity),
        in_specs=[pl.BlockSpec(memory_space=pltpu.VMEM), pl.BlockSpec(memory_space=pltpu.HBM)],
        out_specs=pl.BlockSpec(memory_space=pltpu.HBM),
        out_shape=jax.ShapeDtypeStruct((sources * rows, LANES), BF16),
        scratch_shapes=[
            pltpu.VMEM(arrived.shape, F32),
            pltpu.VMEM((held, slots, width), BF16),
            pltpu.VMEM(weights.shape, BF16),
            pltpu.VMEM((held, slots, LANES), F32),
            pltpu.VMEM((held, slots, LANES), F32),
            pltpu.VMEM((sources * rows, LANES), F32),
            pltpu.VMEM((sources * rows, LANES), BF16),
            pltpu.SemaphoreType.DMA((held, 2)),
            pltpu.SemaphoreType.DMA((8,)),
        ],
        compiler_params=pltpu.CompilerParams(vmem_limit_bytes=50 * MIB),
        cost_estimate=pl.CostEstimate(
            flops=2 * held * slots * labels * width,
            bytes_accessed=2 * held * labels * width,
            transcendentals=held * slots * labels,
        ),
        name="score_labels",
    )(arrived, weights)


def centroid_kernel(spacing, *refs):
    chips = (len(refs) - 7) // 3
    mine_refs, theirs_refs, centroids_ref, out_refs = (
        refs[:chips], refs[chips : 2 * chips], refs[2 * chips], refs[2 * chips + 1 : -6],
    )
    x, w, peak, mass, heads, sems = refs[-6:]
    held = w.shape[0]
    size = held // sems.shape[0]
    block = 512
    pieces = []
    for i in range(sems.shape[0]):
        part = pl.ds(i * size, size)
        pieces.append(pltpu.make_async_copy(centroids_ref.at[part], w.at[part], sems.at[i]))
    ahead = 4
    for copy in pieces[:ahead]:
        copy.start()
    rows = mine_refs[0].shape[0]
    for i in range(chips):
        x[2 * i * rows : (2 * i + 1) * rows, :] = mine_refs[i][...]
        x[(2 * i + 1) * rows : (2 * i + 2) * rows, :] = theirs_refs[i][...]

    def product(first):
        scores = lax.dot_general(
            x[...], w[first : first + block, :], (((1,), (1,)), ((), ())), preferred_element_type=F32
        )
        cuts = [scores[:, j * LANES : (j + 1) * LANES] for j in range(block // LANES)]
        largest = functools.reduce(jnp.maximum, cuts)
        if first > 0:
            before = peak[...]
            largest = jnp.maximum(largest, before)
        summed = sum(jnp.exp(cut - largest) for cut in cuts)
        if first > 0:
            summed = summed + mass[...] * jnp.exp(before - largest)
        peak[...] = largest
        mass[...] = summed
        for h in range(first // spacing, (first + block) // spacing):
            heads[h : h + 1, :] = w[h * spacing : h * spacing + 16, :].astype(F32)[0:1]

    for i, copy in enumerate(pieces):
        copy.wait()
        for later in pieces[i + ahead : i + ahead + 1]:
            later.start()
        for first in range(i * size, (i + 1) * size, block):
            product(first)
    picked = lax.dot_general(x[...], heads[...].astype(BF16), (((1,), (1,)), ((), ())), preferred_element_type=F32)
    largest = jnp.max(peak[...], axis=1, keepdims=True)
    summed = jnp.sum(mass[...] * jnp.exp(peak[...] - largest), axis=1, keepdims=True)
    count = heads.shape[0]
    lane = lax.broadcasted_iota(jnp.int32, peak.shape, 1)
    padded = jnp.concatenate([picked, jnp.zeros((peak.shape[0], LANES - count), F32)], axis=1)
    shares = jnp.where(lane == count, largest, jnp.where(lane == count + 1, summed, padded))
    for i, ref in enumerate(out_refs):
        ref[...] = shares[2 * i * rows : 2 * (i + 1) * rows, :]


def score_centroids(mine, theirs, centroids, spacing):
    rows, width = mine[0].shape
    held = centroids.shape[0]
    chips = len(mine)
    total = 2 * rows * chips
    whole = pl.BlockSpec(memory_space=pltpu.VMEM)
    return pl.pallas_call(
        functools.partial(centroid_kernel, spacing),
        in_specs=[whole] * (2 * chips) + [pl.BlockSpec(memory_space=pltpu.HBM)],
        out_specs=[whole] * chips,
        out_shape=[jax.ShapeDtypeStruct((2 * rows, LANES), F32)] * chips,
        scratch_shapes=[
            pltpu.VMEM((total, width), BF16),
            pltpu.VMEM(centroids.shape, BF16),
            pltpu.VMEM((total, LANES), F32),
            pltpu.VMEM((total, LANES), F32),
            pltpu.VMEM((held // spacing, width), F32),
            pltpu.SemaphoreType.DMA((4,)),
        ],
        compiler_params=pltpu.CompilerParams(vmem_limit_bytes=53 * MIB),
        cost_estimate=pl.CostEstimate(
            flops=2 * total * held * width, bytes_accessed=2 * held * width, transcendentals=total * held
        ),
        name="score_centroids",
    )(*mine, *theirs, centroids)


def prior_kernel(heads, owner_ref, ids_ref, *refs):
    *share_refs, out_ref = refs
    beam, rows, _ = out_ref.shape
    lane = lax.broadcasted_iota(jnp.int32, (rows, LANES), 1)
    shares = [ref[i * rows : (i + 1) * rows, :] for ref in share_refs for i in range(ref.shape[0] // rows)]
    largest = functools.reduce(jnp.maximum, [v[:, heads : heads + 1] for v in shares])
    summed = sum(v[:, heads + 1 : heads + 2] * jnp.exp(v[:, heads : heads + 1] - largest) for v in shares)
    normalizer = largest + jnp.log(summed)
    ids = ids_ref[...]
    for s in range(beam):
        here = jnp.zeros((rows, LANES), F32)
        for o, v in enumerate(shares):
            at = ids[:, s : s + 1] - owner_ref[o] * heads
            here += jnp.where((lane == at) & (lane < heads), v, 0.0)
        picked = jnp.sum(here, axis=1, keepdims=True)
        out_ref[s] = jnp.broadcast_to(picked - normalizer, (rows, LANES))


def priors(owners, ids, shares, heads):
    rows, beam = ids.shape
    whole = pl.BlockSpec(memory_space=pltpu.VMEM)
    return pl.pallas_call(
        functools.partial(prior_kernel, heads),
        in_specs=[pl.BlockSpec(memory_space=pltpu.SMEM)] + [whole] * (1 + len(shares)),
        out_specs=whole,
        out_shape=jax.ShapeDtypeStruct((beam, rows, LANES), F32),
        compiler_params=pltpu.CompilerParams(vmem_limit_bytes=4 * MIB),
        name="priors",
    )(owners, ids, *shares)


def join_kernel(places, columns, row_ref, place_ref, prior_ref, scores_ref, out_ref, totals, wide, ready, sems):
    beam, queries, _ = prior_ref.shape
    rows = places * columns + 2
    sources = scores_ref.shape[0] // rows
    spans = 8
    span = scores_ref.shape[0] // spans
    for i in range(spans):
        wide[i * span : (i + 1) * span, :] = scores_ref[i * span : (i + 1) * span, :].astype(F32)
    terms = wide[pl.ds(places * columns, sources, stride=rows), :]
    for j in range(places):
        total = sum(terms[:, t * places + j : t * places + j + 1] for t in range(3))
        totals[j * sources : (j + 1) * sources, :] = jnp.broadcast_to(total, (sources, LANES))

    parts = sems.shape[0]
    block = queries // parts

    def copy(g):
        here = pl.ds(g * block * beam * columns, block * beam * columns)
        return pltpu.make_async_copy(ready.at[here], out_ref.at[here], sems.at[g])

    for g in range(parts):
        for q in range(g * block, (g + 1) * block):
            for s in range(beam):
                row = wide[pl.ds(row_ref[s, q], columns), :]
                shift = prior_ref[s, q : q + 1, :] - totals[pl.ds(place_ref[s, q], 1), :]
                ready[pl.ds(q * beam * columns + s, columns, stride=beam), :] = row + shift
        copy(g).start()
    for g in range(parts):
        copy(g).wait()


def join(row_of, place_of, prior, scores, places, labels):
    beam, queries = row_of.shape
    columns = labels // LANES
    sources = scores.shape[0] // (places * columns + 2)
    whole = pl.BlockSpec(memory_space=pltpu.VMEM)
    out = pl.pallas_call(
        functools.partial(join_kernel, places, columns),
        in_specs=[pl.BlockSpec(memory_space=pltpu.SMEM)] * 2 + [whole] * 2,
        out_specs=pl.BlockSpec(memory_space=pltpu.HBM),
        out_shape=jax.ShapeDtypeStruct((queries * beam * columns, LANES), F32),
        scratch_shapes=[
            pltpu.VMEM((places * sources, LANES), F32),
            pltpu.VMEM(scores.shape, F32),
            pltpu.VMEM((queries * beam * columns, LANES), F32),
            pltpu.SemaphoreType.DMA((8,)),
        ],
        compiler_params=pltpu.CompilerParams(vmem_limit_bytes=24 * MIB),
        name="join",
    )(row_of, place_of, prior, scores)
    return out.reshape(queries, columns, beam, LANES).transpose(0, 2, 1, 3).reshape(queries, beam, labels)


def exchange(x, axes):
    return lax.all_to_all(x, axes, split_axis=0, concat_axis=0, tiled=True)


def shift(x, by):
    owners = lax.axis_size("own")
    return lax.ppermute(x, "own", [(i, (i + by) % owners) for i in range(owners)])


def swap(x):
    return lax.ppermute(x, "own", [(i, i ^ 1) for i in range(lax.axis_size("own"))])


def body(queries, centroids, cluster_ids, label_weights):
    rows, width = queries.shape
    beam = cluster_ids.shape[1]
    owners = lax.axis_size("own")
    devices = lax.axis_size("grp") * owners
    held, labels, _ = label_weights.shape
    clusters = held * devices
    capacity = 2 * rows * beam // clusters
    spacing = centroids.shape[0] * owners // clusters
    heads = centroids.shape[0] // spacing
    everyone = ("grp", "own")
    hops = range(2, owners, 2)

    mine = [queries] + [shift(queries, by) for by in hops]
    outgoing = route(queries, cluster_ids.T, clusters, capacity)
    outgoing, *mine = lax.optimization_barrier((outgoing, *mine))
    arrived = exchange(outgoing, everyone)

    theirs = [swap(piece) for piece in mine]
    shares = score_centroids(mine, theirs, centroids, spacing)
    arrived, _ = lax.optimization_barrier((arrived, shares[0]))
    back = [shares[0]] + [shift(share, -by) for share, by in zip(shares[1:], hops)]

    scores = score_labels(arrived, label_weights, devices, capacity)
    scores, named, *back = lax.optimization_barrier((scores, cluster_ids.T, *back))
    row_of, place_of = find_places(named, clusters, capacity, held, labels // LANES)
    pairs = labels * held * capacity // LANES // 2 + 1
    scores_home = exchange(scores.reshape(devices, pairs, 2, LANES), everyone).reshape(scores.shape)

    mate = swap(jnp.concatenate([share[rows:] for share in back], axis=0))
    here = lax.axis_index("own")
    steps = jnp.arange(0, owners, 2, dtype=jnp.int32)
    shard = jnp.concatenate([(here + steps) % owners, ((here ^ 1) + steps) % owners]).astype(jnp.int32)
    prior = priors(shard, cluster_ids, [share[:rows] for share in back] + [mate], heads)
    return join(row_of, place_of, prior, scores_home, held * capacity, labels)


def solution(mesh):
    placed = (
        P(("grp", "own"), None),
        P("own", None),
        P(("grp", "own"), None),
        P(("grp", "own"), None, None),
    )
    return jax.shard_map(
        body, mesh=mesh, in_specs=placed, out_specs=P(("grp", "own"), None, None), check_vma=False
    )
```
